256 devices in a mesh: dp: 2 (over core), tp: 2 (over x_lo), seq: 64 (over y, z, x_hi).
Axes of the slice: x: 4 (x_hi: 2, x_lo: 2; x = x_hi * 2 + x_lo), y: 4, z: 8, core: 2. Of those that a mesh axis runs over, the one named last changes fastest.
Arguments:
- query: bfloat16 [2, 8192, 4096], P('dp', 'seq', 'tp'), may hold values from -6 to 6
- keys: bfloat16 [2, 8192, 4096], P('dp', 'seq', 'tp'), may hold values from -6 to 6
- values: bfloat16 [2, 8192, 4096], P('dp', 'seq', 'tp'), may hold values from -6 to 6
- gate_logit: bfloat16 [2, 8192, 4096], P('dp', 'seq', 'tp'), may hold values from -8 to 8
- out_grad: bfloat16 [2, 8192, 4096], P('dp', 'seq', 'tp'), may hold values from -6 to 6
- norm_gain: float32 [4096], P('tp'), may hold values from 0.5 to 1.5
- decay_exp: int32 [32], P('tp'), may hold values from 1 to 16383, as said below
Outputs:
- query_grad: bfloat16 [2, 8192, 4096], P('dp', 'seq', 'tp')
- key_grad: bfloat16 [2, 8192, 4096], P('dp', 'seq', 'tp')
- value_grad: bfloat16 [2, 8192, 4096], P('dp', 'seq', 'tp')
- gate_grad: bfloat16 [2, 8192, 4096], P('dp', 'seq', 'tp')
- gain_grad: float32 [4096], P('tp')
The draws below stay inside these ranges and needn't reach their ends.
Inputs may be any that keep to these rules, and one draw needn't show every extreme that they name: `decay_exp`: the smallest and the largest exponent each belong to some head.
All inputs are finite; a program needn't handle non-finite values.
Results may differ from the reference program's by a relative error of at most 0.0014.
Values sent between devices are 32-bit elements; how exact they have to be, the bound alone decides.
A program may use at most 192 MiB of HBM per device.

```python
import jax
import jax.numpy as jnp
from jax import lax

HEADS = 32
DH = 128
GROUP = 128
LENGTH = 8192
BATCH = 2
COLS = 4096


def draw_decay_exp(key, part):
    key = jax.random.fold_in(key, 7)
    first, second, third = jax.random.split(key, 3)
    top = int(2 * LENGTH).bit_length() - 1
    expo = jax.random.randint(first, (HEADS,), 0, top)
    base = jnp.left_shift(jnp.ones((HEADS,), jnp.int32), expo)
    extra = jax.random.randint(second, (HEADS,), 0, 1 << 30) % base
    result = base + extra
    order = jax.random.permutation(third, HEADS)
    result = result.at[order[0]].set(2 * LENGTH - 1)
    result = result.at[order[1]].set(1)
    return result.astype(jnp.int32)


def level_of(own_key, extent, pieces, low, top_value):
    level, own = 1.0, jax.random.fold_in(own_key, 6)
    for dim, parts in pieces:
        draws = jnp.exp(jax.random.uniform(jax.random.fold_in(own, dim), (parts,), jnp.float32, low / len(pieces), top_value / len(pieces)))
        level = level * jnp.repeat(draws, extent[dim] // parts).reshape([-1 if axis == dim else 1 for axis in range(len(extent))])
    return level


def scatter_about(own_key, shape, scale, reach, shards=(), kind=jnp.bfloat16):
    array = jax.random.normal(own_key, shape, jnp.float32) * scale
    if len(shards) > 0:
        array = level_of(own_key, shape, shards, -0.22, 0.18) * array
    return jnp.clip(array, min=-reach, max=reach).astype(kind)


def setup_inputs(seed: int = 0) -> dict:
    streams_of = jax.random.split(jax.random.key(seed), 8)
    query = scatter_about(streams_of[0], (BATCH, LENGTH, COLS), 1.0, 6.0, ((0, 2), (1, 64), (2, 2)))
    keys = scatter_about(streams_of[1], (BATCH, LENGTH, COLS), 1.0, 6.0, ((0, 2), (1, 64), (2, 2)))
    values = scatter_about(streams_of[2], (BATCH, LENGTH, COLS), 1.0, 6.0, ((0, 2), (1, 64), (2, 2)))
    gate_logit = scatter_about(streams_of[3], (BATCH, LENGTH, COLS), 2.0, 8.0, ((0, 2), (1, 64), (2, 2)))
    out_grad = scatter_about(streams_of[4], (BATCH, LENGTH, COLS), 1.0, 6.0, ((0, 2), (1, 64), (2, 2)))
    norm_gain = jnp.clip(1.0 + 0.1 * jax.random.normal(streams_of[5], (COLS,), jnp.float32), 0.5, 1.5)
    decay_exp = draw_decay_exp(jax.random.fold_in(streams_of[7], 71), 0)
    return dict(query=query, keys=keys, values=values, gate_logit=gate_logit, out_grad=out_grad, norm_gain=norm_gain, decay_exp=decay_exp)


EPS = 1e-06
HIGHEST_ACCURACY = lax.Precision.HIGHEST

def reference(query, keys, values, gate_logit, out_grad, norm_gain, decay_exp):
    nseq = query.shape[0]
    total_len = query.shape[1]
    width = query.shape[2]
    nblock = total_len // GROUP
    rate = -decay_exp.astype(jnp.float32) / (16.0 * LENGTH)
    pos = jnp.arange(GROUP).astype(jnp.float32)
    diff = pos[:, None] - pos[None, :]
    intra = jnp.where((diff >= 0)[None], jnp.exp2(rate[:, None, None] * jnp.maximum(diff, 0.0)[None]), 0.0)
    head_input = jnp.exp2(rate[None, :] * (pos[:, None] + 1.0))
    trailing_output = jnp.exp2(rate[None, :] * (GROUP - pos[:, None]))
    saved_state = jnp.exp2(rate[None, :] * (GROUP - 1.0 - pos[:, None]))
    leading_part = jnp.exp2(rate[None, :] * pos[:, None])
    whole = jnp.exp2(rate * GROUP)

    def blocks(x):
        return x.astype(jnp.float32).reshape(nseq, nblock, GROUP, HEADS, DH).transpose(1, 0, 2, 3, 4)

    def unblock(x):
        return x.transpose(1, 0, 2, 3, 4).reshape(nseq, total_len, width)
    qb = blocks(query)
    kb = blocks(keys)
    vb = blocks(values)

    def forward(state, inputs):
        query_rows, key_rows, value_rows = inputs
        scores = jnp.einsum('bihd,bjhd->bhij', query_rows, key_rows, precision=HIGHEST_ACCURACY) * intra[None]
        output_rows = jnp.einsum('bhij,bjhd->bihd', scores, value_rows, precision=HIGHEST_ACCURACY)
        output_rows = output_rows + head_input[None, :, :, None] * jnp.einsum('bihk,bhkv->bihv', query_rows, state, precision=HIGHEST_ACCURACY)
        new = whole[None, :, None, None] * state + jnp.einsum('bjhk,bjhv->bhkv', saved_state[None, :, :, None] * key_rows, value_rows, precision=HIGHEST_ACCURACY)
        return (new, (output_rows, state))
    zero_state = jnp.zeros((nseq, HEADS, DH, DH), jnp.float32)
    _, (ob, prevs) = lax.scan(forward, zero_state, (qb, kb, vb))
    attn = unblock(ob)
    sig = jax.nn.sigmoid(gate_logit.astype(jnp.float32))
    dy = out_grad.astype(jnp.float32)
    rms = jnp.sqrt(lax.optimization_barrier(jnp.mean(attn * attn, axis=-1, keepdims=True)) + EPS)
    unit = attn / rms
    dn = dy * sig
    gate_grad = (dy * unit * norm_gain * sig * (1.0 - sig)).astype(jnp.bfloat16)
    gain_grad = lax.optimization_barrier(jnp.sum(dn * unit, axis=(0, 1)))
    proj = lax.optimization_barrier(jnp.mean(unit * norm_gain * dn, axis=-1, keepdims=True))
    attention_grad = (norm_gain * dn - unit * proj) / rms
    db = blocks(attention_grad)

    def backward(dstate, inputs):
        query_rows, key_rows, value_rows, dout, preceding_part = inputs
        scores = jnp.einsum('bihd,bjhd->bhij', query_rows, key_rows, precision=HIGHEST_ACCURACY) * intra[None]
        dscores = jnp.einsum('bihd,bjhd->bhij', dout, value_rows, precision=HIGHEST_ACCURACY) * intra[None]
        query_gradient = jnp.einsum('bhij,bjhd->bihd', dscores, key_rows, precision=HIGHEST_ACCURACY)
        query_gradient = query_gradient + head_input[None, :, :, None] * jnp.einsum('bihv,bhkv->bihk', dout, preceding_part, precision=HIGHEST_ACCURACY)
        key_gradient = jnp.einsum('bhij,bihd->bjhd', dscores, query_rows, precision=HIGHEST_ACCURACY)
        key_gradient = key_gradient + trailing_output[None, :, :, None] * jnp.einsum('bjhv,bhkv->bjhk', value_rows, dstate, precision=HIGHEST_ACCURACY)
        value_gradient = jnp.einsum('bhij,bihd->bjhd', scores, dout, precision=HIGHEST_ACCURACY)
        value_gradient = value_gradient + trailing_output[None, :, :, None] * jnp.einsum('bjhk,bhkv->bjhv', key_rows, dstate, precision=HIGHEST_ACCURACY)
        new = whole[None, :, None, None] * dstate + jnp.einsum('bihk,bihv->bhkv', leading_part[None, :, :, None] * query_rows, dout, precision=HIGHEST_ACCURACY)
        return (new, (query_gradient, key_gradient, value_gradient))
    _, (dqb, dkb, dvb) = lax.scan(backward, zero_state, (qb, kb, vb, db, prevs), reverse=True)
    query_grad = unblock(dqb).astype(jnp.bfloat16)
    key_grad = unblock(dkb).astype(jnp.bfloat16)
    value_grad = unblock(dvb).astype(jnp.bfloat16)
    return (query_grad, key_grad, value_grad, gate_grad, gain_grad)
```

```python
import jax
import jax.numpy as jnp
from jax import lax
from jax.experimental import pallas as pl
from jax.experimental.pallas import tpu as pltpu
from jax.sharding import PartitionSpec as P

DH = 128
COLS = 4096
EPS = 1e-06
NY, NZ = 4, 8
NYZ = NY * NZ
HALF = 8
HEADS = 2 * HALF
ROWS = 128
PART = DH // NY
MESH = pl.DeviceIdType.MESH
F32, BF16 = jnp.float32, jnp.bfloat16


def near(i):
    odd = i % 2
    return (odd * ((i + 1) // 2) + (1 - odd) * (NZ - i // 2)) % NZ


def split2(x):
    hi = x.astype(BF16)
    return hi, (x - hi.astype(F32)).astype(BF16)


def nn(a, b):
    return lax.dot_general(a, b, (((1,), (0,)), ((), ())), preferred_element_type=F32)


def nt(a, b):
    return lax.dot_general(a, b, (((1,), (1,)), ((), ())), preferred_element_type=F32)


def lanes(*parts):
    return jnp.concatenate(parts, axis=1)


def stack(*parts):
    return jnp.concatenate(parts, axis=0)


def wait_bytes(ref, sem):
    pltpu.make_async_copy(ref, ref, sem).wait()


def kernel(
    q_hbm, k_hbm, v_hbm, gate_hbm, og_hbm, gain_ref, dec_ref,
    dq_hbm, dk_hbm, dv_hbm, dgate_hbm, dgain_ref,
    q_v, k_v, v_v, gate_v, og_v, in_sem,
    dq_v, dk_v, dv_v, dgate_v, out_sem,
    state_f, rs_f, pair_f, a2a_f, scan_f, ret_f, msg_f, pre_f,
    state_b, rs_b, pair_b, a2a_b, scan_b, ret_b, msg_b, pre_b,
    one_f, many_f, one_b, many_b,
    attn_v, dn_v, gq_v, datt_v, dkf_v, dvf_v,
    acc_v, col_v, st_v, st_sem,
    gz, gy, gx, gd, g_send, g_recv,
):
    seq = lax.axis_index("seq")
    x = seq % 2
    yz = seq // 2
    z = yz % NZ
    y = yz // NZ

    def at_yz(yy, zz):
        return {"seq": (yy * NZ + zz) * 2 + x}

    x_other = {"seq": seq + 1 - 2 * x}
    tp_other = {"tp": 1 - lax.axis_index("tp")}
    dp_index = lax.axis_index("dp")
    dp_other = {"dp": 1 - dp_index}

    barrier = pltpu.get_barrier_semaphore()

    def greet(r, c):
        pl.semaphore_signal(
            barrier, inc=1, device_id={"seq": ((yz + r) % NYZ) * 2 + x}, device_id_type=MESH
        )
        return c

    loads = [
        pltpu.make_async_copy(src.at[0], dst, in_sem.at[n])
        for n, (src, dst) in enumerate(
            ((k_hbm, k_v), (v_hbm, v_v), (q_hbm, q_v), (gate_hbm, gate_v), (og_hbm, og_v))
        )
    ]
    for load in loads:
        load.start()
    lax.fori_loop(1, NYZ, greet, 0)
    for other in (x_other, tp_other, dp_other):
        pl.semaphore_signal(barrier, inc=1, device_id=other, device_id_type=MESH)

    row = lax.broadcasted_iota(jnp.int32, (ROWS, ROWS), 0).astype(F32)
    col = lax.broadcasted_iota(jnp.int32, (ROWS, ROWS), 1).astype(F32)

    def cols(h):
        return pl.ds(pl.multiple_of(h * DH, DH), DH)

    def rate_of(h):
        return dec_ref[h].astype(F32) * (-1.0 / (16.0 * 8192.0))

    def decay(h, n):
        return jnp.exp2(rate_of(h) * n)

    def whole_of(h, blocks):
        return jnp.exp2(jnp.full((1, DH), blocks * float(ROWS), F32) * rate_of(h))

    def remote(src, dst, send, recv, to):
        pltpu.make_async_remote_copy(
            src_ref=src, dst_ref=dst, send_sem=send, recv_sem=recv, device_id=to, device_id_type=MESH
        ).start()

    def send_states(make, state, rs, one, many):
        def turn(i, c):
            hh = (z + near(HALF - 1 - i)) % NZ
            h = HALF * (1 - x) + hh
            state[h] = make(h)
            remote(state.at[h], rs.at[hh], one.at[0], many.at[0, hh], x_other)
            return c

        lax.fori_loop(0, HALF, turn, 0)

    def pairs(make, first, state, rs, pair, a2a, one, many, filler):
        def head(i):
            hh = (z + near(HALF - 1 - i)) % NZ
            h = HALF * x + hh
            state[h] = make(h)
            filler(i)
            wait_bytes(rs.at[hh], many.at[0, hh])
            w = whole_of(h, 1.0)
            mine = jnp.where(first, w, 1.0)
            theirs = jnp.where(first, 1.0, w)
            pair[hh] = mine * state[h] + theirs * rs[hh]
            return hh

        def send(hh, yy):
            remote(
                pair.at[hh, pl.ds(yy * PART, PART)],
                a2a.at[(yz - (yy * NZ + hh) + NYZ) % NYZ],
                one.at[1],
                one.at[2],
                at_yz(yy, hh),
            )

        def turn(i, c):
            hh = head(i)
            for yy in range(NY):
                send(hh, yy)
            return c

        lax.fori_loop(0, HALF - 1, turn, 0)
        head(HALF - 1)
        for r in range(1, NY):
            send(z, (y + r) % NY)
        a2a[0] = pair[z, pl.ds(pl.multiple_of(y * PART, PART), PART)]
        wait_bytes(a2a.at[pl.ds(1, NYZ - 1)], one.at[2])

    def scan(a2a, out, ret, one, many, reverse):
        w2 = whole_of(HALF * x + z, 2.0)
        carry = jnp.zeros((PART, DH), F32)
        for j in reversed(range(NYZ)) if reverse else range(NYZ):
            out[j] = carry
            carry = w2 * carry + a2a[(j - yz + NYZ) % NYZ]

        def send(yy, zz):
            remote(
                out.at[yy * NZ + zz],
                ret.at[z, pl.ds(pl.multiple_of(y * PART, PART), PART)],
                one.at[3],
                many.at[1, z],
                at_yz(yy, zz),
            )

        for r in range(1, NY):
            send((y + r) % NY, z)
        ret[z, pl.ds(pl.multiple_of(y * PART, PART), PART)] = out[yz]

        def turn(i, c):
            zz = (z + near(i)) % NZ
            for yy in range(NY):
                send(yy, zz)
            return c

        lax.fori_loop(1, HALF, turn, 0)

    def spread(first, state, rs, ret, msg, pre, one, many, consume):
        def own(i, size):
            hh = (z + near(i)) % NZ
            h = HALF * x + hh
            wait_bytes(ret.at[hh, pl.ds(0, size)], many.at[1, hh])
            carry = ret[hh]
            after = whole_of(h, 1.0) * carry + jnp.where(first, state[h], rs[hh])
            msg[hh] = jnp.where(first, after, carry)
            remote(msg.at[hh], pre.at[h], one.at[4], many.at[2, hh], x_other)
            pre[h] = jnp.where(first, carry, after)
            consume(h)

        def other(i):
            hh = (z + near(i)) % NZ
            h = HALF * (1 - x) + hh
            wait_bytes(pre.at[h], many.at[2, hh])
            consume(h)

        own(0, DH - PART)

        own(1, DH)

        def turn(i, c):
            own(i, DH)
            other(i - 2)
            return c

        lax.fori_loop(2, HALF, turn, 0)
        other(HALF - 2)
        other(HALF - 1)

    def drain(state, pair, out, msg, one):
        wait_bytes(state.at[pl.ds(0, HALF)], one.at[0])
        wait_bytes(out.at[pl.ds(0, NYZ - 1)], one.at[1])
        wait_bytes(out.at[pl.ds(0, NYZ - 1)], one.at[3])
        wait_bytes(msg, one.at[4])

    def make_state(h):
        kt = k_v[:, cols(h)].T
        hi, lo = split2(v_v[:, cols(h)].astype(F32) * decay(h, ROWS - 1.0 - row))
        return nn(lanes(kt, kt), stack(hi, lo))

    def local_out(h):
        c = cols(h)
        q, k, v = q_v[:, c], k_v[:, c], v_v[:, c]
        keep = jnp.where(row >= col, decay(h, jnp.maximum(row - col, 0.0)), 0.0)
        hi, lo = split2(nt(q, k) * keep)
        attn_v[:, c] = nn(lanes(hi, lo), stack(v, v))
        sig = jax.nn.sigmoid(gate_v[:, c].astype(F32))
        dn = og_v[:, c].astype(F32) * sig
        dn_v[:, c] = dn
        gq_v[:, c] = dn * gain_ref[pl.ds(h, 1), :] * (1.0 - sig)

    def fill_f(i):
        local_out(2 * i)
        local_out(2 * i + 1)

    def consume_f(h):
        c = cols(h)
        q = q_v[:, c]
        hi, lo = split2(pre_f[h])
        out = attn_v[:, c] + decay(h, row + 1.0) * nn(lanes(q, q), stack(hi, lo))
        attn_v[:, c] = out
        acc_v[0] += out * out
        acc_v[1] += out * (dn_v[:, c] * gain_ref[pl.ds(h, 1), :])

    loads[0].wait()
    loads[1].wait()
    pl.semaphore_wait(barrier, NYZ - 1 + 3)
    send_states(make_state, state_f, rs_f, one_f, many_f)
    for load in loads[2:]:
        load.wait()
    acc_v[...] = jnp.zeros_like(acc_v)
    pairs(make_state, x == 0, state_f, rs_f, pair_f, a2a_f, one_f, many_f, fill_f)
    scan(a2a_f, scan_f, ret_f, one_f, many_f, False)
    spread(x == 0, state_f, rs_f, ret_f, msg_f, pre_f, one_f, many_f, consume_f)

    ones = jnp.ones((8, 3 * DH), BF16)
    for n in range(2):
        total = acc_v[n]
        hi, mid = split2(total)
        low = (total - hi.astype(F32) - mid.astype(F32)).astype(BF16)
        st_v[0, pl.ds(8 * n, 8)] = nt(ones, lanes(hi, mid, low))
    sums = pltpu.make_async_remote_copy(
        src_ref=st_v.at[0], dst_ref=st_v.at[1], send_sem=st_sem.at[0], recv_sem=st_sem.at[1],
        device_id=tp_other, device_id_type=MESH,
    )
    sums.start()
    sums.wait()
    both = st_v[0] + st_v[1]
    inv = 1.0 / jnp.sqrt(both[0:8] / COLS + EPS)
    proj = both[8:16] * inv / COLS
    col_v[0] = jnp.broadcast_to(inv[0:1], (ROWS, DH)).T
    col_v[1] = jnp.broadcast_to((proj * inv * inv)[0:1], (ROWS, DH)).T

    def make_cotangent(h):
        c = cols(h)
        attn, dn = attn_v[:, c], dn_v[:, c]
        unit = attn * col_v[0]
        dgate_v[:, c] = (unit * gq_v[:, c]).astype(BF16)
        gz[z, pl.ds(h, 1), :] = jnp.sum(dn * unit, axis=0, keepdims=True)
        datt = dn * gain_ref[pl.ds(h, 1), :] * col_v[0] - attn * col_v[1]
        datt_v[:, c] = datt
        qt = q_v[:, c].T
        hi, lo = split2(decay(h, row) * datt)
        return nn(lanes(qt, qt), stack(hi, lo))

    def local_grads(h):
        c = cols(h)
        q, k, v, datt = q_v[:, c], k_v[:, c], v_v[:, c], datt_v[:, c]
        dhi, dlo = split2(datt)
        keep = jnp.where(row >= col, decay(h, jnp.maximum(row - col, 0.0)), 0.0)
        keep_t = jnp.where(col >= row, decay(h, jnp.maximum(col - row, 0.0)), 0.0)
        dd, vv = lanes(dhi, dlo), lanes(v, v)
        hi, lo = split2(nt(dd, vv) * keep)
        thi, tlo = split2(nt(vv, dd) * keep_t)
        shi, slo = split2(nt(k, q) * keep_t)
        phi, plo = split2(pre_f[h])
        dq = nn(lanes(hi, lo), stack(k, k))
        dq = dq + decay(h, row + 1.0) * nt(lanes(dhi, dlo, dhi), lanes(phi, phi, plo))
        dq_v[:, c] = dq.astype(BF16)
        dkf_v[:, c] = nn(lanes(thi, tlo), stack(q, q))
        dvf_v[:, c] = nn(lanes(shi, slo, shi), stack(dhi, dhi, dlo))

    def other_half(i):
        return HALF * (1 - x) + (z + near(HALF - 1 - i)) % NZ

    def own_half(i):
        return HALF * x + (z + near(HALF - 1 - i)) % NZ

    def fill_b(i):
        local_grads(other_half(i))
        local_grads(own_half(i))

    def consume_b(h):
        c = cols(h)
        k, v = k_v[:, c], v_v[:, c]
        hi, lo = split2(pre_b[h])
        trail = decay(h, ROWS - row)
        dk_v[:, c] = (dkf_v[:, c] + trail * nt(lanes(v, v), lanes(hi, lo))).astype(BF16)
        dv_v[:, c] = (dvf_v[:, c] + trail * nn(lanes(k, k), stack(hi, lo))).astype(BF16)

    send_states(make_cotangent, state_b, rs_b, one_b, many_b)
    pairs(make_cotangent, x == 1, state_b, rs_b, pair_b, a2a_b, one_b, many_b, fill_b)
    stores = [
        pltpu.make_async_copy(src, dst.at[0], out_sem.at[n])
        for n, (src, dst) in enumerate(
            ((dgate_v, dgate_hbm), (dq_v, dq_hbm), (dk_v, dk_hbm), (dv_v, dv_hbm))
        )
    ]
    stores[0].start()
    stores[1].start()
    scan(a2a_b, scan_b, ret_b, one_b, many_b, True)

    for r in range(1, NZ):
        remote(gz.at[z], gz.at[z], g_send.at[0], g_recv.at[0], at_yz(y, (z + r) % NZ))
    wait_bytes(gz.at[pl.ds(0, NZ - 1)], g_recv.at[0])
    total = gz[0]
    for n in range(1, NZ):
        total = total + gz[n]
    gy[y] = total
    for r in range(1, NY):
        remote(gy.at[y], gy.at[y], g_send.at[1], g_recv.at[1], at_yz((y + r) % NY, z))
    spread(x == 1, state_b, rs_b, ret_b, msg_b, pre_b, one_b, many_b, consume_b)
    stores[2].start()
    stores[3].start()
    wait_bytes(gy.at[pl.ds(0, NY - 1)], g_recv.at[1])
    gx[x] = gy[0] + gy[1] + gy[2] + gy[3]
    remote(gx.at[x], gx.at[x], g_send.at[2], g_recv.at[2], x_other)
    wait_bytes(gx.at[0], g_recv.at[2])
    gd[dp_index] = gx[0] + gx[1]
    remote(gd.at[dp_index], gd.at[dp_index], g_send.at[3], g_recv.at[3], dp_other)
    wait_bytes(gd.at[0], g_recv.at[3])
    dgain_ref[...] = gd[0] + gd[1]

    drain(state_f, pair_f, scan_f, msg_f, one_f)
    drain(state_b, pair_b, scan_b, msg_b, one_b)
    wait_bytes(gz.at[pl.ds(0, NZ - 1)], g_send.at[0])
    wait_bytes(gy.at[pl.ds(0, NY - 1)], g_send.at[1])
    wait_bytes(gx.at[0], g_send.at[2])
    wait_bytes(gd.at[0], g_send.at[3])
    for store in stores:
        store.wait()


def per_device(query, keys, values, gate_logit, out_grad, norm_gain, decay_exp):
    rows, width = query.shape[1], query.shape[2]
    wide = jax.ShapeDtypeStruct((1, rows, width), BF16)
    anywhere = pl.BlockSpec(memory_space=pl.ANY)
    vmem = pltpu.VMEM
    flat16 = vmem((rows, width), BF16)
    flat32 = vmem((rows, width), F32)
    comm = [
        vmem((HEADS, DH, DH), F32),
        vmem((HALF, DH, DH), F32),
        vmem((HALF, DH, DH), F32),
        vmem((NYZ, PART, DH), F32),
        vmem((NYZ, PART, DH), F32),
        vmem((HALF, DH, DH), F32),
        vmem((HALF, DH, DH), F32),
        vmem((HEADS, DH, DH), F32),
    ]
    sems = [pltpu.SemaphoreType.DMA((5,)), pltpu.SemaphoreType.DMA((3, HALF))]
    dq, dk, dv, dgate, dgain = pl.pallas_call(
        kernel,
        name="attention_grads",
        out_shape=[wide] * 4 + [jax.ShapeDtypeStruct((HEADS, DH), F32)],
        in_specs=[anywhere] * 5
        + [pl.BlockSpec(memory_space=pltpu.VMEM), pl.BlockSpec(memory_space=pltpu.SMEM)],
        out_specs=[anywhere] * 4 + [pl.BlockSpec(memory_space=pltpu.VMEM)],
        scratch_shapes=[flat16] * 5
        + [pltpu.SemaphoreType.DMA((5,))]
        + [flat16] * 4
        + [pltpu.SemaphoreType.DMA((4,))]
        + comm
        + comm
        + sems
        + sems
        + [flat32] * 6
        + [
            vmem((2, rows, DH), F32),
            vmem((2, rows, DH), F32),
            vmem((2, 16, DH), F32),
            pltpu.SemaphoreType.DMA((2,)),
            vmem((NZ, HEADS, DH), F32),
            vmem((NY, HEADS, DH), F32),
            vmem((2, HEADS, DH), F32),
            vmem((2, HEADS, DH), F32),
            pltpu.SemaphoreType.DMA((4,)),
            pltpu.SemaphoreType.DMA((4,)),
        ],
        compiler_params=pltpu.CompilerParams(
            collective_id=0, has_side_effects=True, vmem_limit_bytes=48 * 2**20
        ),
    )(query, keys, values, gate_logit, out_grad, norm_gain.reshape(HEADS, DH), decay_exp)
    return dq, dk, dv, dgate, dgain.reshape(width)


def solution(mesh):
    wide = P("dp", "seq", "tp")
    return jax.shard_map(
        per_device,
        mesh=mesh,
        in_specs=(wide,) * 5 + (P("tp"),) * 2,
        out_specs=(wide,) * 4 + (P("tp"),),
        check_vma=False,
    )
```

```python
import functools

import jax
import jax.numpy as jnp
from jax import lax
from jax.experimental import pallas as pl
from jax.experimental.pallas import tpu as pltpu
from jax.sharding import PartitionSpec as P

DH = 128
COLS = 4096
EPS = 1e-06
NY, NZ = 4, 8
NYZ = NY * NZ
HALF = 8
HEADS = 2 * HALF
ROWS = 128
BATCHES = 2
BROWS = DH // BATCHES
PART = BROWS // NY
MID_SPREAD = 3
LAG = 8
MESH = pl.DeviceIdType.MESH
F32, BF16 = jnp.float32, jnp.bfloat16


def near(i):
    odd = lax.rem(i, 2)
    return odd * lax.div(i + 1, 2) + (1 - odd) * (NZ - lax.div(i, 2))


def split2(x):
    hi = x.astype(BF16)
    return hi, (x - hi.astype(F32)).astype(BF16)


def nn(a, b):
    return lax.dot_general(a, b, (((1,), (0,)), ((), ())), preferred_element_type=F32)


def nt(a, b):
    return lax.dot_general(a, b, (((1,), (1,)), ((), ())), preferred_element_type=F32)


def lanes(*parts):
    return jnp.concatenate(parts, axis=1)


def stack(*parts):
    return jnp.concatenate(parts, axis=0)


def nothing():
    pass


def wait_bytes(ref, sem):
    pltpu.make_async_copy(ref, ref, sem).wait()


def kernel(
    q_hbm, k_hbm, v_hbm, gate_hbm, og_hbm, gain_ref, dec_ref,
    dq_hbm, dk_hbm, dv_hbm, dgate_hbm, dgain_ref,
    q_v, k_v, v_v, gate_v, og_v, in_sem,
    dq_v, dk_v, dv_v, dgate_v, out_sem,
    state_f, rs_f, pair_f, a2a_f, scan_f, ret_f, msg_f, pre_f,
    state_b, rs_b, pair_b, a2a_b, scan_b, ret_b, msg_b, pre_b,
    one_f, many_f, one_b, many_b,
    attn_v, dn_v, gq_v, datt_v, dkf_v, dvf_v,
    acc_v, col_v, st_v, st_sem,
    gz, gy, gx, gd, g_send, g_recv,
):
    seq = lax.axis_index("seq")
    x = lax.rem(seq, 2)
    yz = lax.div(seq, 2)
    z = lax.rem(yz, NZ)
    y = lax.div(yz, NZ)

    def at_yz(yy, zz):
        return {"seq": (yy * NZ + zz) * 2 + x}

    x_other = {"seq": seq + 1 - 2 * x}
    tp_other = {"tp": 1 - lax.axis_index("tp")}
    dp_index = lax.axis_index("dp")
    dp_other = {"dp": 1 - dp_index}

    barrier = pltpu.get_barrier_semaphore()

    def greet(r, c):
        pl.semaphore_signal(
            barrier, inc=1, device_id={"seq": lax.rem(yz + r, NYZ) * 2 + x}, device_id_type=MESH
        )
        return c

    loads = [
        pltpu.make_async_copy(src.at[0], dst, in_sem.at[n])
        for n, (src, dst) in enumerate(
            ((k_hbm, k_v), (v_hbm, v_v), (q_hbm, q_v), (gate_hbm, gate_v), (og_hbm, og_v))
        )
    ]
    for load in loads:
        load.start()
    lax.fori_loop(1, NYZ, greet, 0)
    for other in (x_other, tp_other, dp_other):
        pl.semaphore_signal(barrier, inc=1, device_id=other, device_id_type=MESH)

    row = lax.broadcasted_iota(jnp.int32, (ROWS, ROWS), 0).astype(F32)
    col = lax.broadcasted_iota(jnp.int32, (ROWS, ROWS), 1).astype(F32)

    def cols(h):
        return pl.ds(pl.multiple_of(h * DH, DH), DH)

    def rate_of(h):
        return dec_ref[h].astype(F32) * (-1.0 / (16.0 * 8192.0))

    def decay(h, n):
        return jnp.exp2(rate_of(h) * n)

    def whole_of(h, blocks):
        return jnp.exp2(jnp.full((1, DH), blocks * float(ROWS), F32) * rate_of(h))

    def remote(src, dst, send, recv, to):
        pltpu.make_async_remote_copy(
            src_ref=src, dst_ref=dst, send_sem=send, recv_sem=recv, device_id=to, device_id_type=MESH
        ).start()

    def own_head(hh):
        return HALF * x + hh

    def other_head(hh):
        return HALF * (1 - x) + hh

    def far(i):
        return lax.rem(z + near(HALF - 1 - i), NZ)

    def close(i):
        return lax.rem(z + NZ - lax.rem(near(i), NZ), NZ)

    def batch_rows(b):
        return pl.ds(BROWS * b, BROWS)

    def part_rows(b, yy):
        return pl.ds(pl.multiple_of(BROWS * b + yy * PART, PART), PART)

    class Scan:
        def __init__(self, make, reverse, state, rs, pair, a2a, out, ret, msg, pre, one, many):
            self.make, self.reverse = make, reverse
            self.state, self.rs, self.pair, self.a2a = state, rs, pair, a2a
            self.out, self.ret, self.msg, self.pre = out, ret, msg, pre
            self.one, self.many = one, many
            self.first = (x == 1) if reverse else (x == 0)

        def send_state(self, b, i):
            hh = far(i)
            r = batch_rows(b)
            remote(
                self.state.at[other_head(hh), r], self.rs.at[hh, r],
                self.one.at[b, 0], self.many.at[0, b, hh], x_other,
            )

        def start(self):
            def turn(i, c):
                h = other_head(far(i))
                self.state[h] = self.make(h)
                self.send_state(0, i)
                return c

            def turn_own(i, c):
                h = own_head(far(i))
                self.state[h] = self.make(h)
                return c

            lax.fori_loop(0, HALF, turn, 0)
            lax.fori_loop(0, HALF, turn_own, 0)

        def combine(self, b, hh):
            r = batch_rows(b)
            wait_bytes(self.rs.at[hh, r], self.many.at[0, b, hh])
            h = own_head(hh)
            w = whole_of(h, 1.0)
            mine = jnp.where(self.first, w, 1.0)
            theirs = jnp.where(self.first, 1.0, w)
            self.pair[hh, r] = mine * self.state[h, r] + theirs * self.rs[hh, r]

        def send_pair(self, b, hh, yy):
            remote(
                self.pair.at[hh, part_rows(b, yy)],
                self.a2a.at[b, lax.rem(yz - (yy * NZ + hh) + NYZ, NYZ)],
                self.one.at[b, 1],
                self.one.at[b, 2],
                at_yz(yy, hh),
            )

        def pairs(self, b, begin, end, filler):
            def turn(i, c):
                hh = far(i)
                if b + 1 < BATCHES:
                    self.send_state(b + 1, i)
                self.combine(b, hh)
                for yy in range(NY):
                    self.send_pair(b, hh, yy)
                filler(b, i)
                return c

            lax.fori_loop(begin, min(end, HALF - 1), turn, 0)
            if end == HALF:
                if b + 1 < BATCHES:
                    self.send_state(b + 1, HALF - 1)
                self.combine(b, z)
                for r in range(1, NY):
                    self.send_pair(b, z, lax.rem(y + r, NY))
                self.a2a[b, 0] = self.pair[z, part_rows(b, y)]
                filler(b, HALF - 1)

        def send_scan(self, b, yy, zz):
            remote(
                self.out.at[b, yy * NZ + zz],
                self.ret.at[z, part_rows(b, y)],
                self.one.at[b, 3],
                self.many.at[1, b, z],
                at_yz(yy, zz),
            )

        def scan(self, b):
            wait_bytes(self.a2a.at[b, pl.ds(1, NYZ - 1)], self.one.at[b, 2])
            w2 = whole_of(own_head(z), 2.0)
            carry = jnp.zeros((PART, DH), F32)
            for j in reversed(range(NYZ)) if self.reverse else range(NYZ):
                self.out[b, j] = carry
                carry = w2 * carry + self.a2a[b, lax.rem(j - yz + NYZ, NYZ)]
            for r in range(1, NY):
                self.send_scan(b, lax.rem(y + r, NY), z)
            self.ret[z, part_rows(b, y)] = self.out[b, yz]

            def turn(i, c):
                zz = lax.rem(z + near(i), NZ)
                for yy in range(NY):
                    self.send_scan(b, yy, zz)
                return c

            lax.fori_loop(1, HALF, turn, 0)

        def own(self, b, i):
            hh = close(i)
            h = own_head(hh)
            r = batch_rows(b)
            size = BROWS - PART if isinstance(i, int) and i == 0 else BROWS
            wait_bytes(self.ret.at[hh, pl.ds(0, size)], self.many.at[1, b, hh])
            carry = self.ret[hh, r]
            added = jnp.where(self.first, self.state[h, r], self.rs[hh, r])
            after = whole_of(h, 1.0) * carry + added
            self.msg[hh, r] = jnp.where(self.first, after, carry)
            remote(
                self.msg.at[hh, r], self.pre.at[h, r],
                self.one.at[b, 4], self.many.at[2, b, hh], x_other,
            )
            self.pre[h, r] = jnp.where(self.first, carry, after)

        def other(self, i):
            hh = close(i)
            for b in range(BATCHES):
                r = batch_rows(b)
                wait_bytes(self.pre.at[other_head(hh), r], self.many.at[2, b, hh])

        def spread(self, b, begin, end):
            def turn(i, c):
                self.own(b, i)
                return c

            if begin == 0:
                self.own(b, 0)
            lax.fori_loop(max(begin, 1), end, turn, 0)

        def run(self, filler, consume, hooks):
            self.start()
            hooks[0]()
            self.pairs(0, 0, HALF, filler)
            self.pairs(1, 0, HALF, filler)
            self.scan(0)
            hooks[1]()
            hooks[2]()
            self.spread(0, 0, MID_SPREAD)
            self.scan(1)
            self.spread(0, MID_SPREAD, HALF)
            hooks[3]()
            for i in range(HALF + LAG):
                if i < HALF:
                    self.own(1, i)
                    consume(own_head(close(i)))
                if i >= LAG:
                    self.other(i - LAG)
                    consume(other_head(close(i - LAG)))
                if i == HALF // 2:
                    hooks[4]()

        def drain(self):
            for b in range(BATCHES):
                wait_bytes(self.pair.at[pl.ds(0, HALF), batch_rows(b)], self.one.at[b, 0])
                wait_bytes(self.out.at[b, pl.ds(0, NYZ - 1)], self.one.at[b, 1])
                wait_bytes(self.out.at[b, pl.ds(0, NYZ - 1)], self.one.at[b, 3])
                wait_bytes(self.msg.at[pl.ds(0, HALF), batch_rows(b)], self.one.at[b, 4])

    def make_state(h):
        kt = k_v[:, cols(h)].T
        hi, lo = split2(v_v[:, cols(h)].astype(F32) * decay(h, ROWS - 1.0 - row))
        return nn(lanes(kt, kt), stack(hi, lo))

    def local_out(h):
        c = cols(h)
        q, k, v = q_v[:, c], k_v[:, c], v_v[:, c]
        keep = jnp.where(row >= col, decay(h, jnp.maximum(row - col, 0.0)), 0.0)
        hi, lo = split2(nt(q, k) * keep)
        attn_v[:, c] = nn(lanes(hi, lo), stack(v, v))
        sig = jax.nn.sigmoid(gate_v[:, c].astype(F32))
        dn = og_v[:, c].astype(F32) * sig
        dn_v[:, c] = dn
        gq_v[:, c] = dn * gain_ref[pl.ds(h, 1), :] * (1.0 - sig)

    def fill_f(b, i):
        local_out(HALF * b + i)

    def consume_f(h):
        c = cols(h)
        q = q_v[:, c]
        hi, lo = split2(pre_f[h])
        out = attn_v[:, c] + decay(h, row + 1.0) * nn(lanes(q, q), stack(hi, lo))
        attn_v[:, c] = out
        acc_v[0] += out * out
        acc_v[1] += out * (dn_v[:, c] * gain_ref[pl.ds(h, 1), :])

    loads[0].wait()
    loads[1].wait()
    pl.semaphore_wait(barrier, NYZ - 1 + 3)
    acc_v[...] = jnp.zeros_like(acc_v)

    def load_rest():
        for load in loads[2:]:
            load.wait()

    forward = Scan(
        make_state, False, state_f, rs_f, pair_f, a2a_f, scan_f, ret_f, msg_f, pre_f, one_f, many_f
    )
    forward.run(fill_f, consume_f, [load_rest, nothing, nothing, nothing, nothing])

    ones = jnp.ones((8, 3 * DH), BF16)
    for n in range(2):
        total = acc_v[n]
        hi, mid = split2(total)
        low = (total - hi.astype(F32) - mid.astype(F32)).astype(BF16)
        st_v[0, pl.ds(8 * n, 8)] = nt(ones, lanes(hi, mid, low))
    sums = pltpu.make_async_remote_copy(
        src_ref=st_v.at[0], dst_ref=st_v.at[1], send_sem=st_sem.at[0], recv_sem=st_sem.at[1],
        device_id=tp_other, device_id_type=MESH,
    )
    sums.start()
    sums.wait()
    both = st_v[0] + st_v[1]
    inv = 1.0 / jnp.sqrt(both[0:8] / COLS + EPS)
    proj = both[8:16] * inv / COLS
    col_v[0] = jnp.broadcast_to(inv[0:1], (ROWS, DH)).T
    col_v[1] = jnp.broadcast_to((proj * inv * inv)[0:1], (ROWS, DH)).T

    def make_cotangent(h):
        c = cols(h)
        attn, dn = attn_v[:, c], dn_v[:, c]
        unit = attn * col_v[0]
        dgate_v[:, c] = (unit * gq_v[:, c]).astype(BF16)
        gz[z, pl.ds(h, 1), :] = jnp.sum(dn * unit, axis=0, keepdims=True)
        datt = dn * gain_ref[pl.ds(h, 1), :] * col_v[0] - attn * col_v[1]
        datt_v[:, c] = datt
        qt = q_v[:, c].T
        hi, lo = split2(decay(h, row) * datt)
        return nn(lanes(qt, qt), stack(hi, lo))

    def local_grads(h):
        c = cols(h)
        q, k, v, datt = q_v[:, c], k_v[:, c], v_v[:, c], datt_v[:, c]
        dhi, dlo = split2(datt)
        keep = jnp.where(row >= col, decay(h, jnp.maximum(row - col, 0.0)), 0.0)
        keep_t = jnp.where(col >= row, decay(h, jnp.maximum(col - row, 0.0)), 0.0)
        dd, vv = lanes(dhi, dlo), lanes(v, v)
        hi, lo = split2(nt(dd, vv) * keep)
        thi, tlo = split2(nt(vv, dd) * keep_t)
        shi, slo = split2(nt(k, q) * keep_t)
        phi, plo = split2(pre_f[h])
        dq = nn(lanes(hi, lo), stack(k, k))
        dq = dq + decay(h, row + 1.0) * nt(lanes(dhi, dlo, dhi), lanes(phi, phi, plo))
        dq_v[:, c] = dq.astype(BF16)
        dkf_v[:, c] = nn(lanes(thi, tlo), stack(q, q))
        dvf_v[:, c] = nn(lanes(shi, slo, shi), stack(dhi, dhi, dlo))

    def fill_b(b, i):
        local_grads(HALF * b + i)

    def consume_b(h):
        c = cols(h)
        k, v = k_v[:, c], v_v[:, c]
        hi, lo = split2(pre_b[h])
        trail = decay(h, ROWS - row)
        dk_v[:, c] = (dkf_v[:, c] + trail * nt(lanes(v, v), lanes(hi, lo))).astype(BF16)
        dv_v[:, c] = (dvf_v[:, c] + trail * nn(lanes(k, k), stack(hi, lo))).astype(BF16)

    stores = [
        pltpu.make_async_copy(src, dst.at[0], out_sem.at[n])
        for n, (src, dst) in enumerate(
            ((dgate_v, dgate_hbm), (dq_v, dq_hbm), (dk_v, dk_hbm), (dv_v, dv_hbm))
        )
    ]

    def gain_start():
        for r in range(1, NZ):
            remote(gz.at[z], gz.at[z], g_send.at[0], g_recv.at[0], at_yz(y, lax.rem(z + r, NZ)))
        stores[0].start()

    def gain_z():
        wait_bytes(gz.at[pl.ds(0, NZ - 1)], g_recv.at[0])
        total = gz[0]
        for n in range(1, NZ):
            total = total + gz[n]
        gy[y] = total
        for r in range(1, NY):
            remote(gy.at[y], gy.at[y], g_send.at[1], g_recv.at[1], at_yz(lax.rem(y + r, NY), z))

    def gain_y():
        wait_bytes(gy.at[pl.ds(0, NY - 1)], g_recv.at[1])
        gx[x] = gy[0] + gy[1] + gy[2] + gy[3]
        remote(gx.at[x], gx.at[x], g_send.at[2], g_recv.at[2], x_other)

    def gain_x():
        wait_bytes(gx.at[0], g_recv.at[2])
        gd[dp_index] = gx[0] + gx[1]
        remote(gd.at[dp_index], gd.at[dp_index], g_send.at[3], g_recv.at[3], dp_other)

    backward = Scan(
        make_cotangent, True, state_b, rs_b, pair_b, a2a_b, scan_b, ret_b, msg_b, pre_b, one_b, many_b
    )
    backward.run(fill_b, consume_b, [gain_start, gain_z, stores[1].start, gain_y, gain_x])
    stores[2].start()
    stores[3].start()
    wait_bytes(gd.at[0], g_recv.at[3])
    dgain_ref[...] = gd[0] + gd[1]

    forward.drain()
    backward.drain()
    wait_bytes(gz.at[pl.ds(0, NZ - 1)], g_send.at[0])
    wait_bytes(gy.at[pl.ds(0, NY - 1)], g_send.at[1])
    wait_bytes(gx.at[0], g_send.at[2])
    wait_bytes(gd.at[0], g_send.at[3])
    for store in stores:
        store.wait()


def copy_kernel(a, b, c, d, e, a_out, b_out, c_out, d_out, e_out):
    for src, dst in ((a, a_out), (b, b_out), (c, c_out), (d, d_out), (e, e_out)):
        dst[...] = src[...]


def per_device(query, keys, values, gate_logit, out_grad, norm_gain, decay_exp):
    rows, width = query.shape[1], query.shape[2]
    wide = jax.ShapeDtypeStruct((1, rows, width), BF16)
    anywhere = pl.BlockSpec(memory_space=pl.ANY)
    vmem = pltpu.VMEM
    flat16 = vmem((rows, width), BF16)
    flat32 = vmem((rows, width), F32)
    comm = [
        vmem((HEADS, DH, DH), F32),
        vmem((HALF, DH, DH), F32),
        vmem((HALF, DH, DH), F32),
        vmem((BATCHES, NYZ, PART, DH), F32),
        vmem((BATCHES, NYZ, PART, DH), F32),
        vmem((HALF, DH, DH), F32),
        vmem((HALF, DH, DH), F32),
        vmem((HEADS, DH, DH), F32),
    ]
    sems = [pltpu.SemaphoreType.DMA((BATCHES, 5)), pltpu.SemaphoreType.DMA((3, BATCHES, HALF))]
    dq, dk, dv, dgate, dgain = pl.pallas_call(
        kernel,
        name="attention_grads",
        out_shape=[wide] * 4 + [jax.ShapeDtypeStruct((HEADS, DH), F32)],
        in_specs=[anywhere] * 5
        + [pl.BlockSpec(memory_space=pltpu.VMEM), pl.BlockSpec(memory_space=pltpu.SMEM)],
        out_specs=[anywhere] * 4 + [pl.BlockSpec(memory_space=pltpu.VMEM)],
        scratch_shapes=[flat16] * 5
        + [pltpu.SemaphoreType.DMA((5,))]
        + [flat16] * 4
        + [pltpu.SemaphoreType.DMA((4,))]
        + comm
        + comm
        + sems
        + sems
        + [flat32] * 6
        + [
            vmem((2, rows, DH), F32),
            vmem((2, rows, DH), F32),
            vmem((2, 16, DH), F32),
            pltpu.SemaphoreType.DMA((2,)),
            vmem((NZ, HEADS, DH), F32),
            vmem((NY, HEADS, DH), F32),
            vmem((2, HEADS, DH), F32),
            vmem((2, HEADS, DH), F32),
            pltpu.SemaphoreType.DMA((4,)),
            pltpu.SemaphoreType.DMA((4,)),
        ],
        compiler_params=pltpu.CompilerParams(
            collective_id=0, has_side_effects=True, vmem_limit_bytes=62 * 2**20
        ),
    )(query, keys, values, gate_logit, out_grad, norm_gain.reshape(HEADS, DH), decay_exp)
    dq, dk, dv, dgate, dgain = pl.pallas_call(
        copy_kernel,
        name="results",
        out_shape=[wide] * 4 + [jax.ShapeDtypeStruct((HEADS, DH), F32)],
        in_specs=[pl.BlockSpec(memory_space=pltpu.VMEM)] * 5,
        out_specs=[pl.BlockSpec(memory_space=pltpu.VMEM)] * 5,
        compiler_params=pltpu.CompilerParams(vmem_limit_bytes=62 * 2**20),
    )(dq, dk, dv, dgate, dgain)
    return dq, dk, dv, dgate, dgain.reshape(width)


def solution(mesh):
    wide = P("dp", "seq", "tp")
    return jax.shard_map(
        per_device,
        mesh=mesh,
        in_specs=(wide,) * 5 + (P("tp"),) * 2,
        out_specs=(wide,) * 4 + (P("tp"),),
        check_vma=False,
    )
```

```python
import functools

import jax
import jax.numpy as jnp
from jax import lax
from jax.experimental import pallas as pl
from jax.experimental.pallas import tpu as pltpu
from jax.sharding import PartitionSpec as P

DH = 128
COLS = 4096
EPS = 1e-06
NY, NZ = 4, 8
NYZ = NY * NZ
HALF = 8
HEADS = 2 * HALF
ROWS = 128
BATCHES = 2
BROWS = DH // BATCHES
PART = BROWS // NY
MID_SPREAD = 3
LAG = 8
MESH = pl.DeviceIdType.MESH
F32, BF16 = jnp.float32, jnp.bfloat16


def near(i):
    odd = lax.rem(i, 2)
    return odd * lax.div(i + 1, 2) + (1 - odd) * (NZ - lax.div(i, 2))


def split2(x):
    hi = x.astype(BF16)
    return hi, (x - hi.astype(F32)).astype(BF16)


def nn(a, b):
    return lax.dot_general(a, b, (((1,), (0,)), ((), ())), preferred_element_type=F32)


def nt(a, b):
    return lax.dot_general(a, b, (((1,), (1,)), ((), ())), preferred_element_type=F32)


def lanes(*parts):
    return jnp.concatenate(parts, axis=1)


def stack(*parts):
    return jnp.concatenate(parts, axis=0)


def nothing():
    pass


def wait_bytes(ref, sem):
    pltpu.make_async_copy(ref, ref, sem).wait()


def kernel(
    q_hbm, k_hbm, v_hbm, gate_hbm, og_hbm, gain_ref, dec_ref,
    dq_hbm, dk_hbm, dv_hbm, dgate_hbm, dgain_ref,
    q_v, k_v, v_v, gate_v, og_v, in_sem,
    dq_v, dk_v, dv_v, dgate_v, out_sem,
    state_f, rs_f, pair_f, a2a_f, scan_f, ret_f, msg_f, pre_f,
    state_b, rs_b, pair_b, a2a_b, scan_b, ret_b, msg_b, pre_b,
    one_f, many_f, one_b, many_b,
    attn_v, dn_v, gq_v, datt_v, dkf_v, dvf_v,
    acc_v, col_v, coef, st_v, st_sem,
    gz, gy, gx, gd, g_send, g_recv,
):
    seq = lax.axis_index("seq")
    x = lax.rem(seq, 2)
    yz = lax.div(seq, 2)
    z = lax.rem(yz, NZ)
    y = lax.div(yz, NZ)

    def at_yz(yy, zz):
        return {"seq": (yy * NZ + zz) * 2 + x}

    x_other = {"seq": seq + 1 - 2 * x}
    tp_other = {"tp": 1 - lax.axis_index("tp")}
    dp_index = lax.axis_index("dp")
    dp_other = {"dp": 1 - dp_index}

    barrier = pltpu.get_barrier_semaphore()

    def greet(r, c):
        pl.semaphore_signal(
            barrier, inc=1, device_id={"seq": lax.rem(yz + r, NYZ) * 2 + x}, device_id_type=MESH
        )
        return c

    loads = [
        pltpu.make_async_copy(src.at[0], dst, in_sem.at[n])
        for n, (src, dst) in enumerate(
            ((k_hbm, k_v), (v_hbm, v_v), (q_hbm, q_v), (gate_hbm, gate_v), (og_hbm, og_v))
        )
    ]
    for load in loads[:2]:
        load.start()
    for r in range(1, NYZ):
        greet(r, 0)
    for other in (x_other, tp_other, dp_other):
        pl.semaphore_signal(barrier, inc=1, device_id=other, device_id_type=MESH)
    for load in loads[2:]:
        load.start()

    row = lax.broadcasted_iota(jnp.int32, (ROWS, ROWS), 0).astype(F32)
    col = lax.broadcasted_iota(jnp.int32, (ROWS, ROWS), 1).astype(F32)

    def cols(h):
        return pl.ds(pl.multiple_of(h * DH, DH), DH)

    def rate_of(h):
        return dec_ref[h].astype(F32) * (-1.0 / (16.0 * 8192.0))

    def decay(h, n):
        return jnp.exp2(rate_of(h) * n)

    def whole_of(h, blocks):
        return jnp.exp2(jnp.full((1, DH), blocks * float(ROWS), F32) * rate_of(h))

    def remote(src, dst, send, recv, to):
        pltpu.make_async_remote_copy(
            src_ref=src, dst_ref=dst, send_sem=send, recv_sem=recv, device_id=to, device_id_type=MESH
        ).start()

    def own_head(hh):
        return HALF * x + hh

    def other_head(hh):
        return HALF * (1 - x) + hh

    def far(i):
        return lax.rem(z + near(HALF - 1 - i), NZ)

    def close(i):
        return lax.rem(z + NZ - lax.rem(near(i), NZ), NZ)

    def batch_rows(b):
        return pl.ds(BROWS * b, BROWS)

    def part_rows(b, yy):
        return pl.ds(pl.multiple_of(BROWS * b + yy * PART, PART), PART)

    class Scan:
        def __init__(self, make, reverse, state, rs, pair, a2a, out, ret, msg, pre, one, many):
            self.make, self.reverse = make, reverse
            self.state, self.rs, self.pair, self.a2a = state, rs, pair, a2a
            self.out, self.ret, self.msg, self.pre = out, ret, msg, pre
            self.one, self.many = one, many
            self.first = (x == 1) if reverse else (x == 0)

        def send_state(self, b, i):
            hh = far(i)
            r = batch_rows(b)
            remote(
                self.state.at[other_head(hh), r], self.rs.at[hh, r],
                self.one.at[b, 0], self.many.at[0, b, hh], x_other,
            )

        def start(self):
            def turn(i, c):
                h = other_head(far(i))
                self.state[h] = self.make(h)
                if not self.reverse:
                    return c
                self.send_state(0, i)
                return c

            def turn_own(i, c):
                h = own_head(far(i))
                self.state[h] = self.make(h)
                return c

            lax.fori_loop(0, HALF, turn, 0)
            if not self.reverse:
                pl.semaphore_wait(barrier, NYZ - 1 + 3)
                for i in range(HALF):
                    self.send_state(0, i)
            for i in range(HALF):
                self.send_state(1, i)
            lax.fori_loop(0, HALF, turn_own, 0)

        def combine(self, b, hh):
            r = batch_rows(b)
            wait_bytes(self.rs.at[hh, r], self.many.at[0, b, hh])
            h = own_head(hh)
            mine = coef[1 if self.reverse else 0, pl.ds(h, 1)]
            theirs = coef[0 if self.reverse else 1, pl.ds(h, 1)]
            self.pair[hh, r] = mine * self.state[h, r] + theirs * self.rs[hh, r]

        def send_pair(self, b, hh, yy):
            remote(
                self.pair.at[hh, part_rows(b, yy)],
                self.a2a.at[b, lax.rem(yz - (yy * NZ + hh) + NYZ, NYZ)],
                self.one.at[b, 1],
                self.one.at[b, 2],
                at_yz(yy, hh),
            )

        def pairs(self, b, begin, end, filler):
            def turn(i, c):
                hh = far(i)
                self.combine(b, hh)
                for yy in (2, 1, 3, 0):
                    self.send_pair(b, hh, lax.rem(y + yy, NY))
                filler(b, i)
                return c

            lax.fori_loop(begin, min(end, HALF - 1), turn, 0)
            if end == HALF:
                self.combine(b, z)
                for r in range(1, NY):
                    self.send_pair(b, z, lax.rem(y + r, NY))
                self.a2a[b, 0] = self.pair[z, part_rows(b, y)]
                filler(b, HALF - 1)

        def send_scan(self, b, yy, zz):
            remote(
                self.out.at[b, yy * NZ + zz],
                self.ret.at[z, part_rows(b, y)],
                self.one.at[b, 3],
                self.many.at[1, b, z],
                at_yz(yy, zz),
            )

        def scan(self, b):
            wait_bytes(self.a2a.at[b, pl.ds(1, NYZ - 1)], self.one.at[b, 2])
            w2 = whole_of(own_head(z), 2.0)
            carry = jnp.zeros((PART, DH), F32)
            for j in reversed(range(NYZ)) if self.reverse else range(NYZ):
                self.out[b, j] = carry
                carry = w2 * carry + self.a2a[b, lax.rem(j - yz + NYZ, NYZ)]
            for r in range(1, NY):
                self.send_scan(b, lax.rem(y + r, NY), z)
            self.ret[z, part_rows(b, y)] = self.out[b, yz]

            def turn(i, c):
                zz = lax.rem(z + near(i), NZ)
                for yy in (2, 1, 3, 0):
                    self.send_scan(b, lax.rem(y + yy, NY), zz)
                return c

            lax.fori_loop(1, HALF, turn, 0)

        def own(self, b, i):
            hh = close(i)
            h = own_head(hh)
            r = batch_rows(b)
            size = BROWS - PART if isinstance(i, int) and i == 0 else BROWS
            wait_bytes(self.ret.at[hh, pl.ds(0, size)], self.many.at[1, b, hh])
            w = coef[2, pl.ds(h, 1)]

            def send(src):
                remote(src, self.pre.at[h, r], self.one.at[b, 4], self.many.at[2, b, hh], x_other)

            @pl.when(self.first)
            def _():
                carry = self.ret[hh, r]
                self.msg[hh, r] = w * carry + self.state[h, r]
                send(self.msg.at[hh, r])
                self.pre[h, r] = carry

            @pl.when(jnp.logical_not(self.first))
            def _():
                send(self.ret.at[hh, r])
                self.pre[h, r] = w * self.ret[hh, r] + self.rs[hh, r]

        def other(self, i):
            hh = close(i)
            for b in range(BATCHES):
                r = batch_rows(b)
                wait_bytes(self.pre.at[other_head(hh), r], self.many.at[2, b, hh])

        def spread(self, b, begin, end):
            def turn(i, c):
                self.own(b, i)
                return c

            if begin == 0:
                self.own(b, 0)
            lax.fori_loop(max(begin, 1), end, turn, 0)

        def run(self, filler, consume, hooks):
            self.start()
            hooks[0]()
            self.pairs(0, 0, HALF, filler)
            self.pairs(1, 0, HALF, filler)
            self.scan(0)
            hooks[1]()
            hooks[2]()
            self.spread(0, 0, MID_SPREAD)
            self.scan(1)
            self.spread(0, MID_SPREAD, HALF)
            hooks[3]()
            for i in range(HALF + LAG):
                if i < HALF:
                    self.own(1, i)
                    consume(own_head(close(i)))
                if i >= LAG:
                    self.other(i - LAG)
                    consume(other_head(close(i - LAG)))
                if i == HALF // 2:
                    hooks[4]()

        def drain(self):
            for b in range(BATCHES):
                wait_bytes(self.pair.at[pl.ds(0, HALF), batch_rows(b)], self.one.at[b, 0])
                wait_bytes(self.out.at[b, pl.ds(0, NYZ - 1)], self.one.at[b, 1])
                wait_bytes(self.out.at[b, pl.ds(0, NYZ - 1)], self.one.at[b, 3])
                wait_bytes(self.msg.at[pl.ds(0, HALF), batch_rows(b)], self.one.at[b, 4])

    def make_state(h):
        kt = k_v[:, cols(h)].T
        hi, lo = split2(v_v[:, cols(h)].astype(F32) * decay(h, ROWS - 1.0 - row))
        return nn(lanes(kt, kt), stack(hi, lo))

    def local_out(h):
        c = cols(h)
        q, k, v = q_v[:, c], k_v[:, c], v_v[:, c]
        keep = jnp.where(row >= col, decay(h, jnp.maximum(row - col, 0.0)), 0.0)
        hi, lo = split2(nt(q, k) * keep)
        attn_v[:, c] = nn(lanes(hi, lo), stack(v, v))
        sig = jax.nn.sigmoid(gate_v[:, c].astype(F32))
        dn = og_v[:, c].astype(F32) * sig
        dn_v[:, c] = dn
        gq_v[:, c] = dn * gain_ref[pl.ds(h, 1), :] * (1.0 - sig)

    def fill_f(b, i):
        local_out(HALF * b + i)

    def consume_f(h):
        c = cols(h)
        q = q_v[:, c]
        hi, lo = split2(pre_f[h])
        out = attn_v[:, c] + decay(h, row + 1.0) * nn(lanes(q, q), stack(hi, lo))
        attn_v[:, c] = out
        acc_v[0] += out * out
        acc_v[1] += out * (dn_v[:, c] * gain_ref[pl.ds(h, 1), :])

    for h in range(HEADS):
        coef[2, pl.ds(h, 1)] = whole_of(h, 1.0)
    coef[0] = jnp.where(x == 0, coef[2], 1.0)
    coef[1] = jnp.where(x == 0, 1.0, coef[2])
    loads[0].wait()
    loads[1].wait()
    acc_v[...] = jnp.zeros_like(acc_v)

    def load_rest():
        for load in loads[2:]:
            load.wait()

    forward = Scan(
        make_state, False, state_f, rs_f, pair_f, a2a_f, scan_f, ret_f, msg_f, pre_f, one_f, many_f
    )
    forward.run(fill_f, consume_f, [load_rest, nothing, nothing, nothing, nothing])

    ones = jnp.ones((8, 3 * DH), BF16)
    for n in range(2):
        total = acc_v[n]
        hi, mid = split2(total)
        low = (total - hi.astype(F32) - mid.astype(F32)).astype(BF16)
        st_v[0, pl.ds(8 * n, 8)] = nt(ones, lanes(hi, mid, low))
    sums = pltpu.make_async_remote_copy(
        src_ref=st_v.at[0], dst_ref=st_v.at[1], send_sem=st_sem.at[0], recv_sem=st_sem.at[1],
        device_id=tp_other, device_id_type=MESH,
    )
    sums.start()
    sums.wait()
    both = st_v[0] + st_v[1]
    inv = 1.0 / jnp.sqrt(both[0:8] / COLS + EPS)
    proj = both[8:16] * inv / COLS
    col_v[0] = jnp.broadcast_to(inv[0:1], (ROWS, DH)).T
    col_v[1] = jnp.broadcast_to((proj * inv * inv)[0:1], (ROWS, DH)).T

    def make_cotangent(h):
        c = cols(h)
        attn, dn = attn_v[:, c], dn_v[:, c]
        unit = attn * col_v[0]
        dgate_v[:, c] = (unit * gq_v[:, c]).astype(BF16)
        gz[z, pl.ds(h, 1), :] = jnp.sum(dn * unit, axis=0, keepdims=True)
        datt = dn * gain_ref[pl.ds(h, 1), :] * col_v[0] - attn * col_v[1]
        datt_v[:, c] = datt
        qt = q_v[:, c].T
        hi, lo = split2(decay(h, row) * datt)
        return nn(lanes(qt, qt), stack(hi, lo))

    def local_grads(h):
        c = cols(h)
        q, k, v, datt = q_v[:, c], k_v[:, c], v_v[:, c], datt_v[:, c]
        dhi, dlo = split2(datt)
        keep = jnp.where(row >= col, decay(h, jnp.maximum(row - col, 0.0)), 0.0)
        keep_t = jnp.where(col >= row, decay(h, jnp.maximum(col - row, 0.0)), 0.0)
        dd, vv = lanes(dhi, dlo), lanes(v, v)
        hi, lo = split2(nt(dd, vv) * keep)
        thi, tlo = split2(nt(vv, dd) * keep_t)
        shi, slo = split2(nt(k, q) * keep_t)
        phi, plo = split2(pre_f[h])
        dq = nn(lanes(hi, lo), stack(k, k))
        dq = dq + decay(h, row + 1.0) * nt(lanes(dhi, dlo, dhi), lanes(phi, phi, plo))
        dq_v[:, c] = dq.astype(BF16)
        dkf_v[:, c] = nn(lanes(thi, tlo), stack(q, q))
        dvf_v[:, c] = nn(lanes(shi, slo, shi), stack(dhi, dhi, dlo))

    def fill_b(b, i):
        local_grads(HALF * b + i)

    def consume_b(h):
        c = cols(h)
        k, v = k_v[:, c], v_v[:, c]
        hi, lo = split2(pre_b[h])
        trail = decay(h, ROWS - row)
        dk_v[:, c] = (dkf_v[:, c] + trail * nt(lanes(v, v), lanes(hi, lo))).astype(BF16)
        dv_v[:, c] = (dvf_v[:, c] + trail * nn(lanes(k, k), stack(hi, lo))).astype(BF16)
        pltpu.make_async_copy(dk_v.at[:, c], dk_hbm.at[0, :, c], out_sem.at[2]).start()
        pltpu.make_async_copy(dv_v.at[:, c], dv_hbm.at[0, :, c], out_sem.at[3]).start()

    stores = [
        pltpu.make_async_copy(src, dst.at[0], out_sem.at[n])
        for n, (src, dst) in enumerate(
            ((dgate_v, dgate_hbm), (dq_v, dq_hbm))
        )
    ]

    def gain_start():
        for r in range(1, NZ):
            remote(gz.at[z], gz.at[z], g_send.at[0], g_recv.at[0], at_yz(y, lax.rem(z + r, NZ)))
        stores[0].start()

    def gain_z():
        wait_bytes(gz.at[pl.ds(0, NZ - 1)], g_recv.at[0])
        total = gz[0]
        for n in range(1, NZ):
            total = total + gz[n]
        gy[y] = total
        for r in range(1, NY):
            remote(gy.at[y], gy.at[y], g_send.at[1], g_recv.at[1], at_yz(lax.rem(y + r, NY), z))

    def gain_y():
        wait_bytes(gy.at[pl.ds(0, NY - 1)], g_recv.at[1])
        gx[x] = gy[0] + gy[1] + gy[2] + gy[3]
        remote(gx.at[x], gx.at[x], g_send.at[2], g_recv.at[2], x_other)

    def gain_x():
        wait_bytes(gx.at[0], g_recv.at[2])
        gd[dp_index] = gx[0] + gx[1]
        remote(gd.at[dp_index], gd.at[dp_index], g_send.at[3], g_recv.at[3], dp_other)

    backward = Scan(
        make_cotangent, True, state_b, rs_b, pair_b, a2a_b, scan_b, ret_b, msg_b, pre_b, one_b, many_b
    )
    backward.run(fill_b, consume_b, [gain_start, gain_z, stores[1].start, gain_y, gain_x])
    wait_bytes(gd.at[0], g_recv.at[3])
    dgain_ref[...] = gd[0] + gd[1]

    forward.drain()
    backward.drain()
    wait_bytes(gz.at[pl.ds(0, NZ - 1)], g_send.at[0])
    wait_bytes(gy.at[pl.ds(0, NY - 1)], g_send.at[1])
    wait_bytes(gx.at[0], g_send.at[2])
    wait_bytes(gd.at[0], g_send.at[3])
    for store in stores:
        store.wait()
    wait_bytes(dk_v, out_sem.at[2])
    wait_bytes(dv_v, out_sem.at[3])


def copy_kernel(a, b, c, d, e, a_out, b_out, c_out, d_out, e_out, wide, narrow, sem_in, sem_out):
    moves = []
    half = ROWS // 2
    for n, (src, dst) in enumerate(((a, a_out), (b, b_out), (c, c_out), (d, d_out))):
        for m in range(2):
            rows = pl.ds(m * half, half)
            moves.append((src.at[0, rows], wide.at[n, rows], dst.at[0, rows]))
    moves.append((e, narrow, e_out))
    reads = [
        pltpu.make_async_copy(src, mid, sem_in.at[n]) for n, (src, mid, _) in enumerate(moves)
    ]
    writes = [
        pltpu.make_async_copy(mid, dst, sem_out.at[n]) for n, (_, mid, dst) in enumerate(moves)
    ]
    for read in reads:
        read.start()
    for read, write in zip(reads, writes):
        read.wait()
        write.start()
    for write in writes:
        write.wait()


def per_device(query, keys, values, gate_logit, out_grad, norm_gain, decay_exp):
    rows, width = query.shape[1], query.shape[2]
    wide = jax.ShapeDtypeStruct((1, rows, width), BF16)
    anywhere = pl.BlockSpec(memory_space=pl.ANY)
    vmem = pltpu.VMEM
    flat16 = vmem((rows, width), BF16)
    flat32 = vmem((rows, width), F32)
    comm = [
        vmem((HEADS, DH, DH), F32),
        vmem((HALF, DH, DH), F32),
        vmem((HALF, DH, DH), F32),
        vmem((BATCHES, NYZ, PART, DH), F32),
        vmem((BATCHES, NYZ, PART, DH), F32),
        vmem((HALF, DH, DH), F32),
        vmem((HALF, DH, DH), F32),
        vmem((HEADS, DH, DH), F32),
    ]
    sems = [pltpu.SemaphoreType.DMA((BATCHES, 5)), pltpu.SemaphoreType.DMA((3, BATCHES, HALF))]
    dq, dk, dv, dgate, dgain = pl.pallas_call(
        kernel,
        name="attention_grads",
        out_shape=[wide] * 4 + [jax.ShapeDtypeStruct((HEADS, DH), F32)],
        in_specs=[anywhere] * 5
        + [pl.BlockSpec(memory_space=pltpu.VMEM), pl.BlockSpec(memory_space=pltpu.SMEM)],
        out_specs=[anywhere] * 4 + [pl.BlockSpec(memory_space=pltpu.VMEM)],
        scratch_shapes=[flat16] * 5
        + [pltpu.SemaphoreType.DMA((5,))]
        + [flat16] * 4
        + [pltpu.SemaphoreType.DMA((4,))]
        + comm
        + comm
        + sems
        + sems
        + [flat32] * 6
        + [
            vmem((2, rows, DH), F32),
            vmem((2, rows, DH), F32),
            vmem((3, HEADS, DH), F32),
            vmem((2, 16, DH), F32),
            pltpu.SemaphoreType.DMA((2,)),
            vmem((NZ, HEADS, DH), F32),
            vmem((NY, HEADS, DH), F32),
            vmem((2, HEADS, DH), F32),
            vmem((2, HEADS, DH), F32),
            pltpu.SemaphoreType.DMA((4,)),
            pltpu.SemaphoreType.DMA((4,)),
        ],
        compiler_params=pltpu.CompilerParams(
            collective_id=0, has_side_effects=True, vmem_limit_bytes=62 * 2**20
        ),
    )(query, keys, values, gate_logit, out_grad, norm_gain.reshape(HEADS, DH), decay_exp)
    dq, dk, dv, dgate, dgain = pl.pallas_call(
        copy_kernel,
        name="results",
        out_shape=[wide] * 4 + [jax.ShapeDtypeStruct((HEADS, DH), F32)],
        in_specs=[anywhere] * 5,
        out_specs=[anywhere] * 5,
        scratch_shapes=[
            vmem((4, rows, width), BF16),
            vmem((HEADS, DH), F32),
            pltpu.SemaphoreType.DMA((9,)),
            pltpu.SemaphoreType.DMA((9,)),
        ],
        compiler_params=pltpu.CompilerParams(vmem_limit_bytes=62 * 2**20),
    )(dq, dk, dv, dgate, dgain)
    return dq, dk, dv, dgate, dgain.reshape(width)


def solution(mesh):
    wide = P("dp", "seq", "tp")
    return jax.shard_map(
        per_device,
        mesh=mesh,
        in_specs=(wide,) * 5 + (P("tp"),) * 2,
        out_specs=(wide,) * 4 + (P("tp"),),
        check_vma=False,
    )
```

```python
import functools

import jax
import jax.numpy as jnp
from jax import lax
from jax.experimental import pallas as pl
from jax.experimental.pallas import tpu as pltpu
from jax.sharding import PartitionSpec as P

DH = 128
COLS = 4096
EPS = 1e-06
NY, NZ = 4, 8
NYZ = NY * NZ
HALF = 8
HEADS = 2 * HALF
ROWS = 128
BATCHES = 2
BROWS = DH // BATCHES
PART = BROWS // NY
MID_SPREAD = 3
LAG = 8
MESH = pl.DeviceIdType.MESH
F32, BF16 = jnp.float32, jnp.bfloat16


def near(i):
    if isinstance(i, int):
        return (i + 1) // 2 if i % 2 else (NZ - i // 2) % NZ
    odd = lax.rem(i, 2)
    return odd * lax.div(i + 1, 2) + (1 - odd) * (NZ - lax.div(i, 2))


def split2(x):
    hi = x.astype(BF16)
    return hi, (x - hi.astype(F32)).astype(BF16)


def nn(a, b):
    return lax.dot_general(a, b, (((1,), (0,)), ((), ())), preferred_element_type=F32)


def nt(a, b):
    return lax.dot_general(a, b, (((1,), (1,)), ((), ())), preferred_element_type=F32)


def lanes(*parts):
    return jnp.concatenate(parts, axis=1)


def stack(*parts):
    return jnp.concatenate(parts, axis=0)


def nothing():
    pass


def wait_bytes(ref, sem):
    pltpu.make_async_copy(ref, ref, sem).wait()


def kernel(
    q_hbm, k_hbm, v_hbm, gate_hbm, og_hbm, gain_ref, dec_ref,
    dq_hbm, dk_hbm, dv_hbm, dgate_hbm, dgain_ref,
    q_v, k_v, v_v, gate_v, og_v, in_sem,
    dq_v, dk_v, dv_v, dgate_v, out_sem,
    state_f, rs_f, pair_f, a2a_f, scan_f, ret_f, msg_f, pre_f,
    state_b, rs_b, pair_b, a2a_b, scan_b, ret_b, msg_b, pre_b,
    one_f, many_f, one_b, many_b,
    attn_v, dn_v, gq_v, datt_v, dkf_v, dvf_v,
    acc_v, col_v, coef, st_v, st_sem,
    gz, gy, gx, gd, g_send, g_recv,
):
    seq = lax.axis_index("seq")
    x = lax.rem(seq, 2)
    yz = lax.div(seq, 2)
    z = lax.rem(yz, NZ)
    y = lax.div(yz, NZ)

    def at_yz(yy, zz):
        return {"seq": (yy * NZ + zz) * 2 + x}

    x_other = {"seq": seq + 1 - 2 * x}
    tp_other = {"tp": 1 - lax.axis_index("tp")}
    dp_index = lax.axis_index("dp")
    dp_other = {"dp": 1 - dp_index}

    barrier = pltpu.get_barrier_semaphore()

    def greet(r, c):
        pl.semaphore_signal(
            barrier, inc=1, device_id={"seq": lax.rem(yz + r, NYZ) * 2 + x}, device_id_type=MESH
        )
        return c

    loads = [
        pltpu.make_async_copy(src.at[0], dst, in_sem.at[n])
        for n, (src, dst) in enumerate(
            ((k_hbm, k_v), (v_hbm, v_v), (q_hbm, q_v), (gate_hbm, gate_v), (og_hbm, og_v))
        )
    ]
    for load in loads[:2]:
        load.start()
    for r in range(1, NYZ):
        greet(r, 0)
    for other in (x_other, tp_other, dp_other):
        pl.semaphore_signal(barrier, inc=1, device_id=other, device_id_type=MESH)
    for load in loads[2:]:
        load.start()

    row = lax.broadcasted_iota(jnp.int32, (ROWS, ROWS), 0).astype(F32)
    col = lax.broadcasted_iota(jnp.int32, (ROWS, ROWS), 1).astype(F32)

    def cols(h):
        return pl.ds(pl.multiple_of(h * DH, DH), DH)

    def rate_of(h):
        return dec_ref[h].astype(F32) * (-1.0 / (16.0 * 8192.0))

    def decay(h, n):
        return jnp.exp2(rate_of(h) * n)

    def whole_of(h, blocks):
        return jnp.exp2(jnp.full((1, DH), blocks * float(ROWS), F32) * rate_of(h))

    def remote(src, dst, send, recv, to):
        pltpu.make_async_remote_copy(
            src_ref=src, dst_ref=dst, send_sem=send, recv_sem=recv, device_id=to, device_id_type=MESH
        ).start()

    def own_head(hh):
        return HALF * x + hh

    def other_head(hh):
        return HALF * (1 - x) + hh

    def far(i):
        return lax.rem(z + near(HALF - 1 - i), NZ)

    def close(i):
        return lax.rem(z + NZ - (near(i) if isinstance(i, int) else lax.rem(near(i), NZ)), NZ)

    def batch_rows(b):
        return pl.ds(BROWS * b, BROWS)

    def part_rows(b, yy):
        return pl.ds(pl.multiple_of(BROWS * b + yy * PART, PART), PART)

    class Scan:
        def __init__(self, make, reverse, state, rs, pair, a2a, out, ret, msg, pre, one, many):
            self.make, self.reverse = make, reverse
            self.state, self.rs, self.pair, self.a2a = state, rs, pair, a2a
            self.out, self.ret, self.msg, self.pre = out, ret, msg, pre
            self.one, self.many = one, many
            self.first = (x == 1) if reverse else (x == 0)

        def send_state(self, b, i):
            hh = far(i)
            r = batch_rows(b)
            remote(
                self.state.at[other_head(hh), r], self.rs.at[hh, r],
                self.one.at[b, 0], self.many.at[0, b, hh], x_other,
            )

        def start(self):
            def turn(i, c):
                h = other_head(far(i))
                self.state[h] = self.make(h)
                if not self.reverse:
                    return c
                self.send_state(0, i)
                return c

            def turn_own(i, c):
                h = own_head(far(i))
                self.state[h] = self.make(h)
                return c

            lax.fori_loop(0, HALF, turn, 0)
            if not self.reverse:
                pl.semaphore_wait(barrier, NYZ - 1 + 3)
                for i in range(HALF):
                    self.send_state(0, i)
            for i in range(HALF):
                self.send_state(1, i)
            lax.fori_loop(0, HALF, turn_own, 0)

        def combine(self, b, hh):
            r = batch_rows(b)
            wait_bytes(self.rs.at[hh, r], self.many.at[0, b, hh])
            h = own_head(hh)
            mine = coef[1 if self.reverse else 0, pl.ds(h, 1)]
            theirs = coef[0 if self.reverse else 1, pl.ds(h, 1)]
            self.pair[hh, r] = mine * self.state[h, r] + theirs * self.rs[hh, r]

        def send_pair(self, b, hh, yy):
            remote(
                self.pair.at[hh, part_rows(b, yy)],
                self.a2a.at[b, lax.rem(yz - (yy * NZ + hh) + NYZ, NYZ)],
                self.one.at[b, 1],
                self.one.at[b, 2],
                at_yz(yy, hh),
            )

        def pairs(self, b, begin, end, filler):
            def turn(i, c):
                hh = far(i)
                self.combine(b, hh)
                for yy in (2, 1, 3, 0):
                    self.send_pair(b, hh, lax.rem(y + yy, NY))
                filler(b, i)
                return c

            lax.fori_loop(begin, min(end, HALF - 1), turn, 0)
            if end == HALF:
                self.combine(b, z)
                for r in range(1, NY):
                    self.send_pair(b, z, lax.rem(y + r, NY))
                self.a2a[b, 0] = self.pair[z, part_rows(b, y)]
                filler(b, HALF - 1)

        def send_scan(self, b, yy, zz):
            remote(
                self.out.at[b, yy * NZ + zz],
                self.ret.at[z, part_rows(b, y)],
                self.one.at[b, 3],
                self.many.at[1, b, z],
                at_yz(yy, zz),
            )

        def scan(self, b):
            wait_bytes(self.a2a.at[b, pl.ds(1, NYZ - 1)], self.one.at[b, 2])
            w2 = whole_of(own_head(z), 2.0)
            carry = jnp.zeros((PART, DH), F32)
            for j in reversed(range(NYZ)) if self.reverse else range(NYZ):
                self.out[b, j] = carry
                carry = w2 * carry + self.a2a[b, lax.rem(j - yz + NYZ, NYZ)]
            for r in range(1, NY):
                self.send_scan(b, lax.rem(y + r, NY), z)
            self.ret[z, part_rows(b, y)] = self.out[b, yz]

            for i in range(1, HALF):
                zz = lax.rem(z + near(i), NZ)
                for yy in (2, 1, 3, 0):
                    self.send_scan(b, lax.rem(y + yy, NY), zz)

        def own(self, b, i):
            hh = close(i)
            h = own_head(hh)
            r = batch_rows(b)
            size = BROWS - PART if isinstance(i, int) and i == 0 else BROWS
            wait_bytes(self.ret.at[hh, pl.ds(0, size)], self.many.at[1, b, hh])
            w = coef[2, pl.ds(h, 1)]

            def send(src):
                remote(src, self.pre.at[h, r], self.one.at[b, 4], self.many.at[2, b, hh], x_other)

            @pl.when(self.first)
            def _():
                carry = self.ret[hh, r]
                self.msg[hh, r] = w * carry + self.state[h, r]
                send(self.msg.at[hh, r])
                self.pre[h, r] = carry

            @pl.when(jnp.logical_not(self.first))
            def _():
                send(self.ret.at[hh, r])
                self.pre[h, r] = w * self.ret[hh, r] + self.rs[hh, r]

        def other(self, i):
            hh = close(i)
            for b in range(BATCHES):
                r = batch_rows(b)
                wait_bytes(self.pre.at[other_head(hh), r], self.many.at[2, b, hh])

        def spread(self, b, begin, end):
            for i in range(begin, end):
                self.own(b, i)

        def run(self, filler, consume, hooks):
            self.start()
            hooks[0]()
            self.pairs(0, 0, HALF, filler)
            self.pairs(1, 0, HALF, filler)
            self.scan(0)
            hooks[1]()
            hooks[2]()
            self.spread(0, 0, MID_SPREAD)
            self.scan(1)
            self.spread(0, MID_SPREAD, HALF)
            hooks[3]()
            for i in range(HALF + LAG):
                if i < HALF:
                    self.own(1, i)
                    consume(own_head(close(i)))
                if i >= LAG:
                    self.other(i - LAG)
                    consume(other_head(close(i - LAG)))
                if i == HALF // 2:
                    hooks[4]()

        def drain(self):
            for b in range(BATCHES):
                wait_bytes(self.pair.at[pl.ds(0, HALF), batch_rows(b)], self.one.at[b, 0])
                wait_bytes(self.out.at[b, pl.ds(0, NYZ - 1)], self.one.at[b, 1])
                wait_bytes(self.out.at[b, pl.ds(0, NYZ - 1)], self.one.at[b, 3])
                wait_bytes(self.msg.at[pl.ds(0, HALF), batch_rows(b)], self.one.at[b, 4])

    def make_state(h):
        kt = k_v[:, cols(h)].T
        hi, lo = split2(v_v[:, cols(h)].astype(F32) * decay(h, ROWS - 1.0 - row))
        return nn(lanes(kt, kt), stack(hi, lo))

    def local_out(h):
        c = cols(h)
        q, k, v = q_v[:, c], k_v[:, c], v_v[:, c]
        keep = jnp.where(row >= col, decay(h, jnp.maximum(row - col, 0.0)), 0.0)
        hi, lo = split2(nt(q, k) * keep)
        attn_v[:, c] = nn(lanes(hi, lo), stack(v, v))
        sig = jax.nn.sigmoid(gate_v[:, c].astype(F32))
        dn = og_v[:, c].astype(F32) * sig
        dn_v[:, c] = dn
        gq_v[:, c] = dn * gain_ref[pl.ds(h, 1), :] * (1.0 - sig)

    def fill_f(b, i):
        local_out(HALF * b + i)

    def consume_f(h):
        c = cols(h)
        q = q_v[:, c]
        hi, lo = split2(pre_f[h])
        out = attn_v[:, c] + decay(h, row + 1.0) * nn(lanes(q, q), stack(hi, lo))
        attn_v[:, c] = out
        acc_v[0] += out * out
        acc_v[1] += out * (dn_v[:, c] * gain_ref[pl.ds(h, 1), :])

    for h in range(HEADS):
        coef[2, pl.ds(h, 1)] = whole_of(h, 1.0)
    coef[0] = jnp.where(x == 0, coef[2], 1.0)
    coef[1] = jnp.where(x == 0, 1.0, coef[2])
    loads[0].wait()
    loads[1].wait()
    acc_v[...] = jnp.zeros_like(acc_v)

    def load_rest():
        for load in loads[2:]:
            load.wait()

    forward = Scan(
        make_state, False, state_f, rs_f, pair_f, a2a_f, scan_f, ret_f, msg_f, pre_f, one_f, many_f
    )
    forward.run(fill_f, consume_f, [load_rest, nothing, nothing, nothing, nothing])

    ones = jnp.ones((8, 3 * DH), BF16)
    for n in range(2):
        total = acc_v[n]
        hi, mid = split2(total)
        low = (total - hi.astype(F32) - mid.astype(F32)).astype(BF16)
        st_v[0, pl.ds(8 * n, 8)] = nt(ones, lanes(hi, mid, low))
    sums = pltpu.make_async_remote_copy(
        src_ref=st_v.at[0], dst_ref=st_v.at[1], send_sem=st_sem.at[0], recv_sem=st_sem.at[1],
        device_id=tp_other, device_id_type=MESH,
    )
    sums.start()
    sums.wait()
    both = st_v[0] + st_v[1]
    inv = 1.0 / jnp.sqrt(both[0:8] / COLS + EPS)
    proj = both[8:16] * inv / COLS
    col_v[0] = jnp.broadcast_to(inv[0:1], (ROWS, DH)).T
    col_v[1] = jnp.broadcast_to((proj * inv * inv)[0:1], (ROWS, DH)).T

    def make_cotangent(h):
        c = cols(h)
        attn, dn = attn_v[:, c], dn_v[:, c]
        unit = attn * col_v[0]
        dgate_v[:, c] = (unit * gq_v[:, c]).astype(BF16)
        gz[z, pl.ds(h, 1), :] = jnp.sum(dn * unit, axis=0, keepdims=True)
        datt = dn * gain_ref[pl.ds(h, 1), :] * col_v[0] - attn * col_v[1]
        datt_v[:, c] = datt
        qt = q_v[:, c].T
        hi, lo = split2(decay(h, row) * datt)
        return nn(lanes(qt, qt), stack(hi, lo))

    def local_grads(h):
        c = cols(h)
        q, k, v, datt = q_v[:, c], k_v[:, c], v_v[:, c], datt_v[:, c]
        dhi, dlo = split2(datt)
        keep = jnp.where(row >= col, decay(h, jnp.maximum(row - col, 0.0)), 0.0)
        keep_t = jnp.where(col >= row, decay(h, jnp.maximum(col - row, 0.0)), 0.0)
        dd, vv = lanes(dhi, dlo), lanes(v, v)
        hi, lo = split2(nt(dd, vv) * keep)
        thi, tlo = split2(nt(vv, dd) * keep_t)
        shi, slo = split2(nt(k, q) * keep_t)
        phi, plo = split2(pre_f[h])
        dq = nn(lanes(hi, lo), stack(k, k))
        dq = dq + decay(h, row + 1.0) * nt(lanes(dhi, dlo, dhi), lanes(phi, phi, plo))
        dq_v[:, c] = dq.astype(BF16)
        dkf_v[:, c] = nn(lanes(thi, tlo), stack(q, q))
        dvf_v[:, c] = nn(lanes(shi, slo, shi), stack(dhi, dhi, dlo))

    def fill_b(b, i):
        local_grads(HALF * b + i)

    def consume_b(h):
        c = cols(h)
        k, v = k_v[:, c], v_v[:, c]
        hi, lo = split2(pre_b[h])
        trail = decay(h, ROWS - row)
        dk_v[:, c] = (dkf_v[:, c] + trail * nt(lanes(v, v), lanes(hi, lo))).astype(BF16)
        dv_v[:, c] = (dvf_v[:, c] + trail * nn(lanes(k, k), stack(hi, lo))).astype(BF16)
        pltpu.make_async_copy(dk_v.at[:, c], dk_hbm.at[0, :, c], out_sem.at[2]).start()
        pltpu.make_async_copy(dv_v.at[:, c], dv_hbm.at[0, :, c], out_sem.at[3]).start()

    stores = [
        pltpu.make_async_copy(src, dst.at[0], out_sem.at[n])
        for n, (src, dst) in enumerate(
            ((dgate_v, dgate_hbm), (dq_v, dq_hbm))
        )
    ]

    def gain_start():
        for r in range(1, NZ):
            remote(gz.at[z], gz.at[z], g_send.at[0], g_recv.at[0], at_yz(y, lax.rem(z + r, NZ)))
        stores[0].start()

    def gain_z():
        wait_bytes(gz.at[pl.ds(0, NZ - 1)], g_recv.at[0])
        total = gz[0]
        for n in range(1, NZ):
            total = total + gz[n]
        gy[y] = total
        for r in range(1, NY):
            remote(gy.at[y], gy.at[y], g_send.at[1], g_recv.at[1], at_yz(lax.rem(y + r, NY), z))

    def gain_y():
        wait_bytes(gy.at[pl.ds(0, NY - 1)], g_recv.at[1])
        gx[x] = gy[0] + gy[1] + gy[2] + gy[3]
        remote(gx.at[x], gx.at[x], g_send.at[2], g_recv.at[2], x_other)

    def gain_x():
        wait_bytes(gx.at[0], g_recv.at[2])
        gd[dp_index] = gx[0] + gx[1]
        remote(gd.at[dp_index], gd.at[dp_index], g_send.at[3], g_recv.at[3], dp_other)

    backward = Scan(
        make_cotangent, True, state_b, rs_b, pair_b, a2a_b, scan_b, ret_b, msg_b, pre_b, one_b, many_b
    )
    backward.run(fill_b, consume_b, [gain_start, gain_z, stores[1].start, gain_y, gain_x])
    wait_bytes(gd.at[0], g_recv.at[3])
    dgain_ref[...] = gd[0] + gd[1]

    forward.drain()
    backward.drain()
    wait_bytes(gz.at[pl.ds(0, NZ - 1)], g_send.at[0])
    wait_bytes(gy.at[pl.ds(0, NY - 1)], g_send.at[1])
    wait_bytes(gx.at[0], g_send.at[2])
    wait_bytes(gd.at[0], g_send.at[3])
    for store in stores:
        store.wait()
    wait_bytes(dk_v, out_sem.at[2])
    wait_bytes(dv_v, out_sem.at[3])


def copy_kernel(a, b, c, d, e, a_out, b_out, c_out, d_out, e_out, wide, narrow, sem_in, sem_out):
    moves = []
    half = ROWS // 2
    for n, (src, dst) in enumerate(((a, a_out), (b, b_out), (c, c_out), (d, d_out))):
        for m in range(2):
            rows = pl.ds(m * half, half)
            moves.append((src.at[0, rows], wide.at[n, rows], dst.at[0, rows]))
    moves.append((e, narrow, e_out))
    reads = [
        pltpu.make_async_copy(src, mid, sem_in.at[n]) for n, (src, mid, _) in enumerate(moves)
    ]
    writes = [
        pltpu.make_async_copy(mid, dst, sem_out.at[n]) for n, (_, mid, dst) in enumerate(moves)
    ]
    for read in reads:
        read.start()
    for read, write in zip(reads, writes):
        read.wait()
        write.start()
    for write in writes:
        write.wait()


def per_device(query, keys, values, gate_logit, out_grad, norm_gain, decay_exp):
    rows, width = query.shape[1], query.shape[2]
    wide = jax.ShapeDtypeStruct((1, rows, width), BF16)
    anywhere = pl.BlockSpec(memory_space=pl.ANY)
    vmem = pltpu.VMEM
    flat16 = vmem((rows, width), BF16)
    flat32 = vmem((rows, width), F32)
    comm = [
        vmem((HEADS, DH, DH), F32),
        vmem((HALF, DH, DH), F32),
        vmem((HALF, DH, DH), F32),
        vmem((BATCHES, NYZ, PART, DH), F32),
        vmem((BATCHES, NYZ, PART, DH), F32),
        vmem((HALF, DH, DH), F32),
        vmem((HALF, DH, DH), F32),
        vmem((HEADS, DH, DH), F32),
    ]
    sems = [pltpu.SemaphoreType.DMA((BATCHES, 5)), pltpu.SemaphoreType.DMA((3, BATCHES, HALF))]
    dq, dk, dv, dgate, dgain = pl.pallas_call(
        kernel,
        name="attention_grads",
        out_shape=[wide] * 4 + [jax.ShapeDtypeStruct((HEADS, DH), F32)],
        in_specs=[anywhere] * 5
        + [pl.BlockSpec(memory_space=pltpu.VMEM), pl.BlockSpec(memory_space=pltpu.SMEM)],
        out_specs=[anywhere] * 4 + [pl.BlockSpec(memory_space=pltpu.VMEM)],
        scratch_shapes=[flat16] * 5
        + [pltpu.SemaphoreType.DMA((5,))]
        + [flat16] * 4
        + [pltpu.SemaphoreType.DMA((4,))]
        + comm
        + comm
        + sems
        + sems
        + [flat32] * 6
        + [
            vmem((2, rows, DH), F32),
            vmem((2, rows, DH), F32),
            vmem((3, HEADS, DH), F32),
            vmem((2, 16, DH), F32),
            pltpu.SemaphoreType.DMA((2,)),
            vmem((NZ, HEADS, DH), F32),
            vmem((NY, HEADS, DH), F32),
            vmem((2, HEADS, DH), F32),
            vmem((2, HEADS, DH), F32),
            pltpu.SemaphoreType.DMA((4,)),
            pltpu.SemaphoreType.DMA((4,)),
        ],
        compiler_params=pltpu.CompilerParams(
            collective_id=0, has_side_effects=True, vmem_limit_bytes=62 * 2**20
        ),
    )(query, keys, values, gate_logit, out_grad, norm_gain.reshape(HEADS, DH), decay_exp)
    dq, dk, dv, dgate, dgain = pl.pallas_call(
        copy_kernel,
        name="results",
        out_shape=[wide] * 4 + [jax.ShapeDtypeStruct((HEADS, DH), F32)],
        in_specs=[anywhere] * 5,
        out_specs=[anywhere] * 5,
        scratch_shapes=[
            vmem((4, rows, width), BF16),
            vmem((HEADS, DH), F32),
            pltpu.SemaphoreType.DMA((9,)),
            pltpu.SemaphoreType.DMA((9,)),
        ],
        compiler_params=pltpu.CompilerParams(vmem_limit_bytes=62 * 2**20),
    )(dq, dk, dv, dgate, dgain)
    return dq, dk, dv, dgate, dgain.reshape(width)


def solution(mesh):
    wide = P("dp", "seq", "tp")
    return jax.shard_map(
        per_device,
        mesh=mesh,
        in_specs=(wide,) * 5 + (P("tp"),) * 2,
        out_specs=(wide,) * 4 + (P("tp"),),
        check_vma=False,
    )
```
